32 devices in a mesh: gy: 8 (over z, core), gx: 4 (over y, x).
Axes of the slice: x: 2, y: 2, z: 4, core: 2. Of those that a mesh axis runs over, the one named last changes fastest.
Arguments:
- ice_mask: int32 [512, 1024], P('gy', 'gx'), may hold values 0 or 1
- grounded: int32 [512, 1024], P('gy', 'gx'), may hold values 0 or 1
- thickness: float32 [512, 1024], P('gy', 'gx'), may hold values from 0.25 to 6
- friction: float32 [512, 1024], P('gy', 'gx'), may hold values from 0.3 to 3
- previous_velocity: float32 [2, 512, 1024], P(None, 'gy', 'gx'), may hold values from -6 to 6
- observed: float32 [2, 512, 1024], P(None, 'gy', 'gx'), may hold values from -6 to 6
- driving: float32 [2, 512, 1024], P(None, 'gy', 'gx'), may hold values from -6 to 6
Outputs:
- velocity: float32 [2, 512, 1024], P(None, 'gy', 'gx')
- adjoint: float32 [2, 512, 1024], P(None, 'gy', 'gx')
- friction_gradient: float32 [512, 1024], P('gy', 'gx')
The draws below stay inside these ranges and needn't reach their ends.
All inputs are finite; a program needn't handle non-finite values. No bound on the sum of `ice_mask` or of `grounded` on one device may be relied on, other than what follows from the above.
Results may differ from the reference program's by a relative error of at most 0.00025.
Values sent between devices are 32-bit elements; how exact they have to be, the bound alone decides.
No kernel may reach another device: no remote copies, remote signals or barrier semaphores. Data moves between devices by JAX's collectives and lax.ppermute only.
A program may use at most 64 MiB of HBM per device.

```python
import math
import jax
import jax.numpy as jnp

ITERS = 2
NY = 512
NX = 1024


def draw_thickness(key, part):
    key = jax.random.fold_in(key, 1)
    rows = jnp.arange(NY, dtype=jnp.float32)[:, None]
    ramp = 1.0 + 2.0 * rows / max(NY - 1, 1)
    factor = jnp.exp(jax.random.uniform(key, (NY, NX), jnp.float32, jnp.log(0.5), jnp.log(2.0)))
    return jnp.clip(ramp * factor, 0.25, 6.0).astype(jnp.float32)


def place_ends(values, key, low, high):
    spot = [jax.random.randint(jax.random.fold_in(key, axis), (), 0, length) for axis, length in enumerate(values.shape)]
    longest = values.shape.index(max(values.shape))
    beside = spot[:longest] + [(spot[longest] + 1) % values.shape[longest]] + spot[longest + 1:]
    return values.at[tuple(spot)].set(low).at[tuple(beside)].set(high)


def level_of(stream_key, extent, shards, low, high):
    gain = 1.0
    for axis_at, shards_of in shards:
        steps = jax.random.uniform(jax.random.fold_in(jax.random.fold_in(stream_key, 6), axis_at), (shards_of,), jnp.float32, low / len(shards), high / len(shards))
        gain = gain * jnp.repeat(jnp.exp(steps), extent[axis_at] // shards_of).reshape((-1,) + (1,) * (len(extent) - 1 - axis_at))
    return gain


def noise(own_key, shape, deviation, reach, split=(), held_as=jnp.bfloat16):
    drawn = deviation * jax.random.normal(own_key, shape, jnp.float32)
    if split:
        drawn = drawn * level_of(own_key, shape, split, -0.22, 0.18)
    return jnp.clip(drawn, -reach, reach).astype(held_as)


def setup_inputs(seed: int = 0) -> dict:
    key_of = jax.random.split(jax.random.key(seed), 8)
    ice_mask = place_ends((jax.random.randint(key_of[0], (NY, NX), 0, 8) < 7).astype(jnp.int32), jax.random.fold_in(key_of[0], 1), 0, 1)
    grounded = place_ends((jax.random.randint(key_of[1], (NY, NX), 0, 2) < 1).astype(jnp.int32), jax.random.fold_in(key_of[1], 1), 0, 1)
    thickness = draw_thickness(jax.random.fold_in(key_of[7], 71), 0)
    friction = jnp.clip(jnp.exp(math.log(3.0) - 2.3025851 * jax.random.uniform(key_of[3], (NY, NX), jnp.float32) ** level_of(key_of[3], (NY, NX), ((0, 8), (1, 4)), -0.2, 0.2)), 0.3, 3.0)
    previous_velocity = noise(key_of[4], (2, NY, NX), 1.0, 6.0, ((1, 8), (2, 4)), jnp.float32)
    observed = noise(key_of[5], (2, NY, NX), 1.0, 6.0, ((1, 8), (2, 4)), jnp.float32)
    driving = noise(key_of[6], (2, NY, NX), 1.0, 6.0, ((1, 8), (2, 4)), jnp.float32)
    return {"ice_mask": ice_mask, "grounded": grounded, "thickness": thickness, "friction": friction, "previous_velocity": previous_velocity, "observed": observed, "driving": driving}


def corner_dx(padded):
    return 0.5 * (padded[..., :-1, 1:] - padded[..., :-1, :-1] + padded[..., 1:, 1:] - padded[..., 1:, :-1])


def corner_dy(padded):
    return 0.5 * (padded[..., 1:, :-1] - padded[..., :-1, :-1] + padded[..., 1:, 1:] - padded[..., :-1, 1:])


def back_dx(stress):
    return 0.5 * (-stress[1:, 1:] + stress[1:, :-1] - stress[:-1, 1:] + stress[:-1, :-1])


def back_dy(stress):
    return 0.5 * (-stress[1:, 1:] - stress[1:, :-1] + stress[:-1, 1:] + stress[:-1, :-1])


def corner_weight(padded_vel, padded_thick):
    ux = corner_dx(padded_vel[0])
    uy = corner_dy(padded_vel[0])
    vx = corner_dx(padded_vel[1])
    vy = corner_dy(padded_vel[1])
    strain = ux * ux + vy * vy + ux * vy + 0.25 * (uy + vx) ** 2
    viscous = 0.5 * (strain + 0.01) ** (-1.0 / 3.0)
    mean_thick = 0.25 * (padded_thick[:-1, :-1] + padded_thick[:-1, 1:] + padded_thick[1:, :-1] + padded_thick[1:, 1:])
    return mean_thick * viscous


def stress_div(padded, weight):
    ux = corner_dx(padded[0])
    uy = corner_dy(padded[0])
    vx = corner_dx(padded[1])
    vy = corner_dy(padded[1])
    s_ux = weight * (4.0 * ux + 2.0 * vy)
    s_vy = weight * (4.0 * vy + 2.0 * ux)
    s_shear = weight * (uy + vx)
    div_u = back_dx(s_ux) + back_dy(s_shear)
    div_v = back_dx(s_shear) + back_dy(s_vy)
    return jnp.stack([div_u, div_v], 0)


def reference(ice_mask, grounded, thickness, friction, previous_velocity, observed, driving):
    mask = ice_mask.astype(jnp.float32)
    fric = grounded.astype(jnp.float32) * friction
    start = mask * previous_velocity
    hm = mask * thickness
    weight = corner_weight(jnp.pad(start, ((0, 0), (1, 1), (1, 1))), jnp.pad(hm, 1))

    def operate(field):
        masked = mask * field
        div = stress_div(jnp.pad(masked, ((0, 0), (1, 1), (1, 1))), weight)
        return mask * (div + fric * masked) + (1.0 - mask) * field

    def solve(solution, resid):
        image = operate(resid)
        norm_now = jnp.sum(resid * resid)
        alpha = norm_now / jnp.sum(resid * image)
        direction, along = resid, image
        for step in range(ITERS):
            solution = solution + alpha * direction
            resid = resid - alpha * along
            if step + 1 < ITERS:
                image = operate(resid)
                norm_next = jnp.sum(resid * resid)
                product = jnp.sum(resid * image)
                ratio = norm_next / norm_now
                alpha = norm_next / (product - ratio * norm_next / alpha)
                direction = resid + ratio * direction
                along = image + ratio * along
                norm_now = norm_next
        return solution

    velocity = solve(start, mask * driving - operate(start))
    adjoint = solve(jnp.zeros_like(start), mask * (start - observed))
    gradient = -mask * fric * (velocity[0] * adjoint[0] + velocity[1] * adjoint[1])
    return velocity, adjoint, gradient
```

```python
import functools

import jax
import jax.numpy as jnp
from jax import lax
from jax.experimental import pallas as pl
from jax.experimental.pallas import tpu as pltpu
from jax.sharding import PartitionSpec as P

LANES = 128
TILE = 8
BELOW = 3
ABOVE = 2
SLOT = BELOW
FIELDS = 8
GROUPS = LANES // (SLOT * FIELDS)
VMEM_LIMIT = 32 * 1024 * 1024


def derive(ice, grounded, thick, fric, prev, obs, drv):
    mask = ice.astype(jnp.float32)
    start_u = mask * prev[0]
    start_v = mask * prev[1]
    coef = mask * (grounded.astype(jnp.float32) * fric) + (1.0 - mask)
    return (
        start_u,
        start_v,
        mask * thick,
        coef,
        mask * drv[0],
        mask * drv[1],
        mask * (start_u - obs[0]),
        mask * (start_v - obs[1]),
    )


def read(refs, at):
    return [r[at, :] if len(r.shape) == 2 else r[:, at, :] for r in refs]


def pack_rows_kernel(*refs):
    raw, (down, up), held, arrived = refs[:7], refs[7:9], refs[9:16], refs[16]
    copies = [pltpu.make_async_copy(src, dst, arrived.at[i]) for i, (src, dst) in enumerate(zip(raw, held))]
    for copy in copies:
        copy.start()
    for copy in copies:
        copy.wait()
    rows = held[0].shape[0]
    for f, field in enumerate(derive(*read(held, pl.ds(0, TILE)))):
        up[BELOW * f : BELOW * (f + 1), :] = field[:BELOW]
    for f, field in enumerate(derive(*read(held, pl.ds(rows - TILE, TILE)))):
        down[ABOVE * f : ABOVE * (f + 1), :] = field[TILE - ABOVE :]


def add_columns(blocks, tile, fields):
    group, at_row, lane = *divmod(tile, blocks["tiles"]), blocks["lane"]
    for f, (first, last) in enumerate(fields):
        at = SLOT * (FIELDS * group + f)
        mine = (lane >= at) & (lane < at + ABOVE)
        east = pltpu.roll(last, (at + ABOVE) % LANES, 1)
        blocks["east"][at_row] = jnp.where(mine, east, blocks["east"][at_row])
        mine = (lane >= at) & (lane < at + BELOW)
        west = pltpu.roll(first, at % LANES, 1)
        blocks["west"][at_row] = jnp.where(mine, west, blocks["west"][at_row])


def new_blocks(east, west):
    lane = lax.broadcasted_iota(jnp.int32, (TILE, LANES), 1)
    return {"tiles": len(east), "lane": lane, "east": east, "west": west}


def block_tiles(rows):
    return -(-(rows // TILE + 1) // GROUPS)


def fields_kernel(*refs):
    raw = refs[:7]
    own, east, west = refs[7:]
    rows, cols = own.shape[1:]
    count = block_tiles(rows)
    none = jnp.zeros((TILE, LANES), jnp.float32)
    blocks = new_blocks([none] * count, [none] * count)
    for tile in range(rows // TILE):
        at = pl.ds(TILE * tile, TILE)
        fields = derive(*read(raw, at))
        for f, field in enumerate(fields):
            own[f, at, :] = field
        add_columns(blocks, tile, [(x[:, :LANES], x[:, cols - LANES :]) for x in fields])
    for i in range(count):
        at = pl.ds(TILE * i, TILE)
        east[at, :], west[at, :] = blocks["east"][i], blocks["west"][i]


def tail_kernel(own_tiles, above, below, east_own, west_own, tail, sends):
    cols = tail.shape[2]
    height = east_own.shape[0]
    for f in range(FIELDS):
        tail[f, 0:BELOW, :] = below[BELOW * f : BELOW * (f + 1), :]
        tail[f, BELOW : TILE - ABOVE, :] = jnp.zeros((TILE - ABOVE - BELOW, cols), jnp.float32)
        tail[f, TILE - ABOVE : TILE, :] = above[ABOVE * f : ABOVE * (f + 1), :]
    at = [pl.ds(TILE * i, TILE) for i in range(height // TILE)]
    blocks = new_blocks([east_own[a, :] for a in at], [west_own[a, :] for a in at])
    add_columns(blocks, own_tiles, [(tail[f, :, :LANES], tail[f, :, cols - LANES :]) for f in range(FIELDS)])
    gx, count = lax.axis_index("gx"), lax.axis_size("gx")
    for i in range(count):
        to_next, to_previous = gx + 1 == i, gx - 1 == i
        for j in range(height // TILE):
            block = jnp.where(to_next, blocks["east"][j], jnp.where(to_previous, blocks["west"][j], 0.0))
            sends[pl.ds(height * i + TILE * j, TILE), :] = block


def to_right(x):
    return pltpu.roll(x, x.shape[1] - 1, 1)


def to_left(x):
    return pltpu.roll(x, 1, 1)


def gradient(u0, u1, v0, v1):
    us, ud = u1 + u0, u1 - u0
    vs, vd = v1 + v0, v1 - v0
    ux = to_right(us) - us
    uy = to_right(ud) + ud
    vx = to_right(vs) - vs
    vy = to_right(vd) + vd
    return ux, uy, vx, vy


def stress_of(weight, ux, vy, shear):
    return weight * (4.0 * ux + 2.0 * vy), weight * (4.0 * vy + 2.0 * ux), weight * shear


def solve_kernel(own, tail, columns, out, sums, fld, wgt, wown, strs, res, img, grd):
    rows, cols = own.shape[1:]
    wide = cols + LANES
    ring = rows + TILE
    tiles = ring // TILE
    gy, gx = lax.axis_index("gy"), lax.axis_index("gx")

    lane = lax.broadcasted_iota(jnp.int32, (TILE, LANES), 1)
    from_right, from_left = lane < BELOW, lane >= LANES - ABOVE
    count = block_tiles(rows)
    gx_last = lax.axis_size("gx") - 1
    before = jnp.maximum(gx - 1, 0) * (TILE * count)
    after = jnp.minimum(gx + 1, gx_last) * (TILE * count)
    left, right = [], []
    for i in range(count):
        block = columns[pl.ds(pl.multiple_of(before + TILE * i, TILE), TILE), :]
        left.append(jnp.where(gx > 0, block, 0.0))
        block = columns[pl.ds(pl.multiple_of(after + TILE * i, TILE), TILE), :]
        right.append(jnp.where(gx < gx_last, block, 0.0))
    for t in range(tiles):
        at = pl.ds(TILE * t, TILE)
        group, i = divmod(t, count)
        for f in range(FIELDS):
            lanes = SLOT * (FIELDS * group + f)
            body = own[f, at, :] if t < tiles - 1 else tail[f]
            side = jnp.where(from_left, pltpu.roll(left[i], (2 * LANES - ABOVE - lanes) % LANES, 1), 0.0)
            side = jnp.where(from_right, pltpu.roll(right[i], (LANES - lanes) % LANES, 1), side)
            fld[f, at, :cols] = body
            fld[f, at, cols:] = side
    for f in range(3):
        fld[f, ring : ring + 1, :] = fld[f, 0:1, :]

    def pair(ref, f, t):
        return ref[f, pl.ds(TILE * t, TILE), :], ref[f, pl.ds(TILE * t + 1, TILE), :]

    def put_stress(which, t, parts):
        for i, part in enumerate(parts):
            strs[3 * which + i, pl.ds(TILE * t + TILE, TILE), :] = part
            if t == tiles - 1:
                strs[3 * which + i, TILE - 1 : TILE, :] = part[TILE - 1 :, :]

    def divergence(which, t):
        ux0, vy0, sh0 = [strs[3 * which + i, pl.ds(TILE * t + TILE, TILE), :] for i in range(3)]
        ux1, vy1, sh1 = [strs[3 * which + i, pl.ds(TILE * t + TILE - 1, TILE), :] for i in range(3)]
        a, b = ux0 + ux1, sh1 - sh0
        div_u = (b - a) + to_left(a + b)
        a, b = sh0 + sh1, vy1 - vy0
        div_v = (b - a) + to_left(a + b)
        return div_u, div_v

    def operator(which, t, u, v):
        at = pl.ds(TILE * t, TILE)
        ice = fld[2, at, :] > 0.0
        coef = fld[3, at, :]
        div_u, div_v = divergence(which, t)
        return jnp.where(ice, div_u, 0.0) + coef * u, jnp.where(ice, div_v, 0.0) + coef * v

    row_of = lax.broadcasted_iota(jnp.int32, (TILE, wide), 0)
    col_of = lax.broadcasted_iota(jnp.int32, (TILE, wide), 1)
    own_col = (col_of < cols) | ((col_of == wide - 1) & (gx == 0))
    own_tail = own_col & (row_of == TILE - 1) & (gy == 0)

    for t in range(tiles):
        at = pl.ds(TILE * t, TILE)
        ux, uy, vx, vy = gradient(*pair(fld, 0, t), *pair(fld, 1, t))
        h0, h1 = pair(fld, 2, t)
        hs = h0 + h1
        hs = hs + to_right(hs)
        shear = uy + vx
        strain = ux * ux + vy * vy + ux * vy + 0.25 * (shear * shear)
        weight = (hs * 0.03125) * jnp.exp(jnp.log(0.25 * strain + 0.01) * (-1.0 / 3.0))
        wgt[at, :] = weight
        wown[at, :] = jnp.where(own_col if t < tiles - 1 else own_tail, weight, 0.0)
        put_stress(0, t, stress_of(weight, ux, vy, shear))

    for t in range(tiles):
        at = pl.ds(TILE * t, TILE)
        image = operator(0, t, fld[0, at, :], fld[1, at, :])
        for i in range(2):
            res[i, at, :] = fld[4 + i, at, :] - image[i]
            res[2 + i, at, :] = fld[6 + i, at, :]
    for i in range(4):
        res[i, ring : ring + 1, :] = res[i, 0:1, :]

    for t in range(tiles):
        at = pl.ds(TILE * t, TILE)
        weight = wgt[at, :]
        for s in range(2):
            ux, uy, vx, vy = gradient(*pair(res, 2 * s, t), *pair(res, 2 * s + 1, t))
            shear = uy + vx
            grd[3 * s, at, :], grd[3 * s + 1, at, :], grd[3 * s + 2, at, :] = ux, vy, shear
            put_stress(s, t, stress_of(weight, ux, vy, shear))
    dots = [jnp.zeros((TILE, cols), jnp.float32) for _ in range(4)]
    for t in range(tiles):
        at = pl.ds(TILE * t, TILE)
        for s in range(2):
            r = [res[2 * s + i, at, :] for i in range(2)]
            q = operator(s, t, *r)
            for i in range(2):
                img[2 * s + i, at, :] = q[i]
                if t < tiles - 1:
                    r_own, q_own = r[i][:, :cols], q[i][:, :cols]
                    out[4 * s + i, at, :] = r_own
                    out[4 * s + 2 + i, at, :] = q_own
                    dots[2 * s] = dots[2 * s] + r_own * r_own
                    dots[2 * s + 1] = dots[2 * s + 1] + r_own * q_own
    for i in range(4):
        img[i, ring : ring + 1, :] = img[i, 0:1, :]

    def total(x):
        return jnp.sum(jnp.sum(x, axis=0, keepdims=True), axis=1, keepdims=True)

    dots = [total(x) for x in dots]
    theta = []
    for s in range(2):
        some = dots[2 * s] > 0.0
        theta.append(jnp.where(some, dots[2 * s + 1] / jnp.where(some, dots[2 * s], 1.0), 0.0))

    size = [jnp.zeros((TILE, cols), jnp.float32) for _ in range(2)]
    cells = [[jnp.zeros((TILE, cols), jnp.float32) for _ in range(3)] for _ in range(2)]
    energy = [[jnp.zeros((TILE, wide), jnp.float32) for _ in range(3)] for _ in range(2)]
    for t in range(tiles):
        at = pl.ds(TILE * t, TILE)
        weight = wown[at, :]
        for s in range(2):
            ux, uy, vx, vy = gradient(*pair(img, 2 * s, t), *pair(img, 2 * s + 1, t))
            rx, ry, rs = [grd[3 * s + i, at, :] for i in range(3)]
            wx, wy, ws = ux - theta[s] * rx, vy - theta[s] * ry, (uy + vx) - theta[s] * rs
            sx, sy, ss = stress_of(weight, wx, wy, ws)
            energy[s][0] = energy[s][0] + (sx * wx + sy * wy + ss * ws)
            energy[s][1] = energy[s][1] + (sx * rx + sy * ry + ss * rs)
            sx, sy, ss = stress_of(weight, rx, ry, rs)
            energy[s][2] = energy[s][2] + (sx * rx + sy * ry + ss * rs)
            if t < tiles - 1:
                coef = fld[3, at, :cols]
                for i in range(2):
                    r = res[2 * s + i, at, :cols]
                    w = img[2 * s + i, at, :cols] - theta[s] * r
                    size[s] = size[s] + w * w
                    cells[s][0] = cells[s][0] + coef * (w * w)
                    cells[s][1] = cells[s][1] + coef * (w * r)
                    cells[s][2] = cells[s][2] + coef * (r * r)
    values = []
    for s in range(2):
        values += [dots[2 * s], dots[2 * s + 1], total(size[s])]
        values += [total(energy[s][i]) + total(cells[s][i]) for i in range(3)]
    lane = lax.broadcasted_iota(jnp.int32, (1, LANES), 1)
    row = jnp.zeros((1, LANES), jnp.float32)
    for i, value in enumerate(values):
        row = jnp.where(lane == i, value, row)
    sums[...] = jnp.broadcast_to(row, sums.shape)


def steps_of(table, first):
    norm_d, prod_d, size_d, ww, rw, rr = [table[:, first + i : first + i + 1] for i in range(6)]

    def over(x):
        return jnp.sum(x, axis=0, keepdims=True)

    norm, prod = over(norm_d), over(prod_d)
    alpha = norm / prod
    theta = prod / norm
    some = norm_d > 0.0
    shift = jnp.where(some, prod_d / jnp.where(some, norm_d, 1.0), 0.0) - theta
    square = alpha * alpha
    norm_1 = square * over(size_d + shift * shift * norm_d)
    prod_1 = square * over(ww + shift * (2.0 * rw + shift * rr))
    ratio = norm_1 / norm
    some = norm_1 > 0.0
    bottom = jnp.where(some, prod_1 - ratio * norm_1 / alpha, 1.0)
    return alpha, ratio, norm_1 / bottom


def finish_kernel(table, own, vectors, velocity, adjoint, grad):
    steps = [steps_of(table[...], 6 * s) for s in range(2)]
    rows = own.shape[1]
    for row in range(0, rows, TILE):
        at = pl.ds(row, TILE)
        made = []
        for s in range(2):
            alpha, ratio, alpha_1 = steps[s]
            for i in range(2):
                r, q = vectors[4 * s + i, at, :], vectors[4 * s + 2 + i, at, :]
                step = alpha * r + alpha_1 * ((r - alpha * q) + ratio * r)
                made.append(own[i, at, :] + step if s == 0 else step)
        friction = jnp.where(own[2, at, :] > 0.0, own[3, at, :], 0.0)
        velocity[0, at, :], velocity[1, at, :] = made[0], made[1]
        adjoint[0, at, :], adjoint[1, at, :] = made[2], made[3]
        grad[at, :] = -friction * (made[0] * made[2] + made[1] * made[3])


def shape(*dims):
    return jax.ShapeDtypeStruct(dims, jnp.float32)


def call(kernel, outs, scratch=(), **kwargs):
    return pl.pallas_call(
        kernel,
        out_shape=outs,
        scratch_shapes=scratch,
        compiler_params=pltpu.CompilerParams(vmem_limit_bytes=VMEM_LIMIT),
        **kwargs,
    )


def swap(to_next, to_previous, axis):
    count = lax.axis_size(axis)
    ahead = [(i, i + 1) for i in range(count - 1)]
    back = [(i + 1, i) for i in range(count - 1)]
    return lax.ppermute(to_next, axis, ahead), lax.ppermute(to_previous, axis, back)


def shards(ice_mask, grounded, thickness, friction, previous_velocity, observed, driving):
    raw = (ice_mask, grounded, thickness, friction, previous_velocity, observed, driving)
    rows, cols = ice_mask.shape
    wide, ring = cols + LANES, rows + TILE
    devices = lax.axis_size(("gy", "gx"))
    height = TILE * block_tiles(rows)
    down, up, *held = call(
        pack_rows_kernel,
        (shape(ABOVE * FIELDS, cols), shape(BELOW * FIELDS, cols), *[jax.ShapeDtypeStruct(x.shape, x.dtype) for x in raw]),
        scratch=(pltpu.SemaphoreType.DMA((len(raw),)),),
        in_specs=[pl.BlockSpec(memory_space=pltpu.HBM)] * len(raw),
        name="pack_rows",
    )(*[pltpu.with_memory_space_constraint(x, pltpu.HBM) for x in raw])
    above, below = swap(down, up, "gy")
    own, east_own, west_own = call(
        fields_kernel,
        (shape(FIELDS, rows, cols), shape(height, LANES), shape(height, LANES)),
        name="fields",
        cost_estimate=pl.CostEstimate(flops=40 * rows * cols, bytes_accessed=18 * 4 * rows * cols, transcendentals=0),
    )(*held)
    tail, sends = call(
        functools.partial(tail_kernel, rows // TILE),
        (shape(FIELDS, TILE, cols), shape(lax.axis_size("gx") * height, LANES)),
        name="tail",
    )(above, below, east_own, west_own)
    columns = lax.all_to_all(sends, "gx", 0, 0, tiled=True)
    vectors, sums = call(
        solve_kernel,
        (shape(8, rows, cols), shape(devices, LANES)),
        scratch=(
            pltpu.VMEM((FIELDS, ring + TILE, wide), jnp.float32),
            pltpu.VMEM((ring, wide), jnp.float32),
            pltpu.VMEM((ring, wide), jnp.float32),
            pltpu.VMEM((6, ring + TILE, wide), jnp.float32),
            pltpu.VMEM((4, ring + TILE, wide), jnp.float32),
            pltpu.VMEM((4, ring + TILE, wide), jnp.float32),
            pltpu.VMEM((6, ring, wide), jnp.float32),
        ),
        name="solve",
    )(own, tail, columns)
    table = lax.all_to_all(sums, ("gy", "gx"), 0, 0, tiled=True)
    return call(
        finish_kernel,
        (shape(2, rows, cols), shape(2, rows, cols), shape(rows, cols)),
        name="finish",
    )(table, own, vectors)


def solution(mesh):
    flat, both = P("gy", "gx"), P(None, "gy", "gx")
    return jax.shard_map(
        shards,
        mesh=mesh,
        in_specs=(flat, flat, flat, flat, both, both, both),
        out_specs=(both, both, flat),
        check_vma=False,
    )
```

```python
import jax
import jax.numpy as jnp
from jax import lax
from jax.experimental import pallas as pl
from jax.experimental.pallas import tpu as pltpu
from jax.sharding import PartitionSpec as P

LANES = 128
TILE = 8
BELOW = 3
ABOVE = 2
FROM_LEFT = (2, 2, 2, 1, 1, 1, 2, 2)
FROM_RIGHT = (3, 3, 3, 1, 2, 2, 1, 1)
SLOT = 16
FIELDS = 8
GROUPS = LANES // SLOT
EDGE_TOP = 2
EDGE_BOTTOM = 3
SUMS = 7
SOLVE = 2
VMEM_LIMIT = 32 * 1024 * 1024


def derive(ice, grounded, thick, fric, prev, obs, drv):
    mask = ice.astype(jnp.float32)
    start_u = mask * prev[0]
    start_v = mask * prev[1]
    coef = mask * (grounded.astype(jnp.float32) * fric) + (1.0 - mask)
    return (
        start_u,
        start_v,
        mask * thick,
        coef,
        mask * drv[0],
        mask * drv[1],
        mask * (start_u - obs[0]),
        mask * (start_v - obs[1]),
    )


def read(refs, at):
    return [r[at, :] if len(r.shape) == 2 else r[:, at, :] for r in refs]


def add_columns(blocks, tile, fields):
    group, at_row, lane = *divmod(tile, blocks["tiles"]), blocks["lane"]
    east_at = west_at = SLOT * group
    for f, (first, last) in enumerate(fields):
        mine = (lane >= east_at) & (lane < east_at + FROM_LEFT[f])
        east = pltpu.roll(last, (east_at + FROM_LEFT[f]) % LANES, 1)
        blocks["east"][at_row] = jnp.where(mine, east, blocks["east"][at_row])
        if f in (4, 5):
            first = jnp.where(lane == 1, first - fields[3][0] * fields[f - 4][0], first)
        mine = (lane >= west_at) & (lane < west_at + FROM_RIGHT[f])
        west = pltpu.roll(first, west_at % LANES, 1)
        blocks["west"][at_row] = jnp.where(mine, west, blocks["west"][at_row])
        east_at, west_at = east_at + FROM_LEFT[f], west_at + FROM_RIGHT[f]


def new_blocks(east, west):
    lane = lax.broadcasted_iota(jnp.int32, (TILE, LANES), 1)
    return {"tiles": len(east), "lane": lane, "east": east, "west": west}


def block_tiles(rows):
    return -(-(rows // TILE) // GROUPS)


def pack_kernel(*refs):
    raw, (own, sends), held, arrived = refs[:7], refs[7:9], refs[9:16], refs[16]
    copies = [pltpu.make_async_copy(src, dst, arrived.at[i]) for i, (src, dst) in enumerate(zip(raw, held))]
    for copy in copies:
        copy.start()
    for copy in copies:
        copy.wait()
    rows, cols = own.shape[1:]
    height = block_tiles(rows)
    none = jnp.zeros((TILE, LANES), jnp.float32)
    blocks = new_blocks([none] * height, [none] * height)
    for tile in range(rows // TILE):
        at = pl.ds(TILE * tile, TILE)
        fields = derive(*read(held, at))
        for f, field in enumerate(fields):
            own[f, at, :] = field
        add_columns(blocks, tile, [(x[:, :LANES], x[:, cols - LANES :]) for x in fields])
    gx, count = lax.axis_index("gx"), lax.axis_size("gx")
    for i in range(count):
        to_next, to_previous = gx + 1 == i, gx - 1 == i
        for j in range(height):
            block = jnp.where(to_next, blocks["east"][j], jnp.where(to_previous, blocks["west"][j], 0.0))
            sends[pl.ds(TILE * (height * i + j), TILE), :] = block


def side_columns(columns, rows):
    gx, last = lax.axis_index("gx"), lax.axis_size("gx") - 1
    height = block_tiles(rows)
    lane = lax.broadcasted_iota(jnp.int32, (TILE, LANES), 1)

    def blocks(device, there):
        first = jnp.clip(device, 0, last) * (TILE * height)
        at = [pl.ds(pl.multiple_of(first + TILE * i, TILE), TILE) for i in range(height)]
        return [jnp.where(there, columns[a, :], 0.0) for a in at]

    left, right = blocks(gx - 1, gx > 0), blocks(gx + 1, gx < last)

    def side(f, tile):
        group, i = divmod(tile, height)
        before, after = FROM_LEFT[f], FROM_RIGHT[f]
        at = SLOT * group + sum(FROM_LEFT[:f])
        lanes = jnp.where(lane >= LANES - before, pltpu.roll(left[i], (2 * LANES - before - at) % LANES, 1), 0.0)
        at = SLOT * group + sum(FROM_RIGHT[:f])
        return jnp.where(lane < after, pltpu.roll(right[i], (LANES - at) % LANES, 1), lanes)

    return side


def rows_kernel(own, columns, ends, across, beside):
    rows, cols = own.shape[1:]
    last = rows // TILE - 1
    side = side_columns(columns, rows)
    even = lax.rem(lax.axis_index("gy"), 2) == 0
    for f in range(FIELDS):
        for tile, at in ((last, 0), (0, TILE)):
            ends[f, at : at + TILE, :cols] = own[f, TILE * tile : TILE * (tile + 1), :]
            ends[f, at : at + TILE, cols:] = side(f, tile)
        bottom, top = ends[f, TILE - BELOW : TILE, :], ends[f, TILE : TILE + BELOW, :]
        across[BELOW * f : BELOW * (f + 1), :] = jnp.where(even, top, bottom)
        beside[BELOW * f : BELOW * (f + 1), :] = jnp.where(even, bottom, top)


def to_right(x):
    return pltpu.roll(x, x.shape[1] - 1, 1)


def to_left(x):
    return pltpu.roll(x, 1, 1)


def gradient(u0, u1, v0, v1):
    us, ud = u1 + u0, u1 - u0
    vs, vd = v1 + v0, v1 - v0
    ux = to_right(us) - us
    uy = to_right(ud) + ud
    vx = to_right(vs) - vs
    vy = to_right(vd) + vd
    return ux, uy, vx, vy


def stress_of(weight, ux, vy, shear):
    return weight * (4.0 * ux + 2.0 * vy), weight * (4.0 * vy + 2.0 * ux), weight * shear


def fold(x):
    return sum(x[:, at : at + LANES] for at in range(0, x.shape[1], LANES))


def total(x):
    return jnp.sum(jnp.sum(x, axis=0, keepdims=True), axis=1, keepdims=True)


def sweep(scratch, own_corners, own_rows, theta, put):
    fld, wgt, strs, res, img, grd = scratch
    tiles = len(own_corners)
    wide = fld.shape[2]
    cols = wide - LANES
    blank = jnp.zeros((1, wide), jnp.float32)
    for ref, count, at in ((fld, 3, TILE * tiles), (res, 4, TILE * tiles), (img, 4, TILE * tiles), (strs, 9, TILE - 1)):
        for f in range(count):
            ref[f, at : at + 1, :] = blank

    def pair(ref, f, t):
        return ref[f, pl.ds(TILE * t, TILE), :], ref[f, pl.ds(TILE * t + 1, TILE), :]

    def put_stress(which, t, parts):
        for i, part in enumerate(parts):
            strs[3 * which + i, pl.ds(TILE * t + TILE, TILE), :] = part

    def operator(which, t, u, v):
        ux0, vy0, sh0 = [strs[3 * which + i, pl.ds(TILE * t + TILE, TILE), :] for i in range(3)]
        ux1, vy1, sh1 = [strs[3 * which + i, pl.ds(TILE * t + TILE - 1, TILE), :] for i in range(3)]
        a, b = ux0 + ux1, sh1 - sh0
        div_u = (b - a) + to_left(a + b)
        a, b = sh0 + sh1, vy1 - vy0
        div_v = (b - a) + to_left(a + b)
        at = pl.ds(TILE * t, TILE)
        ice, coef = fld[2, at, :] > 0.0, fld[3, at, :]
        return jnp.where(ice, div_u, 0.0) + coef * u, jnp.where(ice, div_v, 0.0) + coef * v

    for t in range(tiles):
        at = pl.ds(TILE * t, TILE)
        ux, uy, vx, vy = gradient(*pair(fld, 0, t), *pair(fld, 1, t))
        h0, h1 = pair(fld, 2, t)
        hs = h0 + h1
        hs = hs + to_right(hs)
        shear = uy + vx
        strain = ux * ux + vy * vy + ux * vy + 0.25 * (shear * shear)
        weight = (hs * 0.03125) * jnp.exp(jnp.log(0.25 * strain + 0.01) * (-1.0 / 3.0))
        wgt[at, :] = weight
        put_stress(0, t, stress_of(weight, ux, vy, shear))

    for t in range(tiles):
        at = pl.ds(TILE * t, TILE)
        image = operator(0, t, fld[0, at, :], fld[1, at, :])
        for i in range(2):
            res[i, at, :] = fld[4 + i, at, :] - image[i]
            res[2 + i, at, :] = fld[6 + i, at, :]

    for t in range(tiles):
        at = pl.ds(TILE * t, TILE)
        weight = wgt[at, :]
        for s in range(2):
            ux, uy, vx, vy = gradient(*pair(res, 2 * s, t), *pair(res, 2 * s + 1, t))
            shear = uy + vx
            grd[3 * s, at, :], grd[3 * s + 1, at, :], grd[3 * s + 2, at, :] = ux, vy, shear
            put_stress(1 + s, t, stress_of(weight, ux, vy, shear))
    dots = [jnp.zeros((TILE, cols), jnp.float32) for _ in range(4)]
    for t in range(tiles):
        at = pl.ds(TILE * t, TILE)
        for s in range(2):
            r = [res[2 * s + i, at, :] for i in range(2)]
            q = operator(1 + s, t, *r)
            for i in range(2):
                img[2 * s + i, at, :] = q[i]
                r_own, q_own = r[i][:, :cols], q[i][:, :cols]
                put(t, 4 * s + i, r_own)
                put(t, 4 * s + 2 + i, q_own)
                if own_rows[t] is not None:
                    r_own = jnp.where(own_rows[t], r_own, 0.0)
                dots[2 * s] = dots[2 * s] + r_own * r_own
                dots[2 * s + 1] = dots[2 * s + 1] + r_own * q_own
    dots = [fold(x) for x in dots]
    if theta is None:
        theta = []
        for s in range(2):
            norm, prod = total(dots[2 * s]), total(dots[2 * s + 1])
            some = norm > 0.0
            theta.append(jnp.where(some, prod / jnp.where(some, norm, 1.0), 0.0))

    size = [[jnp.zeros((TILE, cols), jnp.float32) for _ in range(2)] for _ in range(2)]
    energy = [[jnp.zeros((TILE, wide), jnp.float32) for _ in range(3)] for _ in range(2)]
    drag = [[jnp.zeros((TILE, cols), jnp.float32) for _ in range(3)] for _ in range(2)]
    for t in range(tiles):
        at = pl.ds(TILE * t, TILE)
        for s in range(2):
            weight = jnp.where(own_corners[t][s], wgt[at, :], 0.0)
            ux, uy, vx, vy = gradient(*pair(img, 2 * s, t), *pair(img, 2 * s + 1, t))
            rx, ry, rs = [grd[3 * s + i, at, :] for i in range(3)]
            wx, wy, ws = ux - theta[s] * rx, vy - theta[s] * ry, (uy + vx) - theta[s] * rs
            sx, sy, ss = stress_of(weight, wx, wy, ws)
            energy[s][0] = energy[s][0] + (sx * wx + sy * wy + ss * ws)
            energy[s][1] = energy[s][1] + (sx * rx + sy * ry + ss * rs)
            sx, sy, ss = stress_of(weight, rx, ry, rs)
            energy[s][2] = energy[s][2] + (sx * rx + sy * ry + ss * rs)
            coef = fld[3, at, :cols]
            for i in range(2):
                r = res[2 * s + i, at, :cols]
                w = img[2 * s + i, at, :cols] - theta[s] * r
                if own_rows[t] is not None:
                    r, w = jnp.where(own_rows[t], r, 0.0), jnp.where(own_rows[t], w, 0.0)
                ww, wr = w * w, w * r
                size[s][0], size[s][1] = size[s][0] + ww, size[s][1] + wr
                drag[s][0] = drag[s][0] + coef * ww
                drag[s][1] = drag[s][1] + coef * wr
                drag[s][2] = drag[s][2] + coef * (r * r)
    sums = []
    for s in range(2):
        sums += [dots[2 * s], dots[2 * s + 1], fold(size[s][0]), fold(size[s][1])]
        sums += [fold(energy[s][i]) + fold(drag[s][i]) for i in range(3)]
    return sums, theta


def own_columns(wide):
    col = lax.broadcasted_iota(jnp.int32, (TILE, wide), 1)
    cols = wide - LANES
    gx, end = lax.axis_index("gx"), lax.axis_size("gx") - 1
    inside, left, right = col < cols - 1, col == wide - 1, col == cols - 1
    return inside | right | (left & (gx == 0)), inside | left | (right & (gx == end))


def row_masks(wide, first, last):
    row = lax.broadcasted_iota(jnp.int32, (TILE, wide), 0)
    rows = (row >= first) & (row <= last)
    return rows, rows[:, : wide - LANES]


def inner_kernel(own, columns, vectors, partial, theta, *scratch):
    fld = scratch[0]
    rows, cols = own.shape[1:]
    wide, tiles = cols + LANES, rows // TILE
    side = side_columns(columns, rows)
    for f in range(FIELDS):
        for t in range(tiles):
            at = pl.ds(TILE * t, TILE)
            fld[f, at, :cols] = own[f, at, :]
            fld[f, at, cols:] = side(f, t)
    corners, cells = [own_columns(wide)] * tiles, [None] * tiles
    for t, first, last in ((0, EDGE_TOP, TILE - 1), (tiles - 1, 0, TILE - 1 - EDGE_BOTTOM)):
        all_lanes, cells[t] = row_masks(wide, first, last)
        corners[t] = [x & all_lanes for x in corners[t]]

    def put(t, which, value):
        vectors[which, TILE * t : TILE * (t + 1), :] = value

    sums, thetas = sweep(scratch, corners, cells, None, put)
    for i, x in enumerate(sums):
        partial[i] = x
    for i, x in enumerate(thetas):
        theta[i] = jnp.broadcast_to(x, (TILE, LANES))


def outer_kernel(ends, across, beside, partial, theta, edges, sums, *scratch):
    fld = scratch[0]
    wide = ends.shape[2]
    even = lax.rem(lax.axis_index("gy"), 2) == 0
    kept = TILE - BELOW
    for f in range(FIELDS):
        a, b = across[BELOW * f : BELOW * (f + 1), :], beside[BELOW * f : BELOW * (f + 1), :]
        below, above = jnp.where(even, b, a), jnp.where(even, a, b)
        fld[f, 0:kept, :] = ends[f, TILE - kept : TILE, :]
        fld[f, kept:TILE, :] = below
        fld[f, TILE : TILE + ABOVE, :] = above[BELOW - ABOVE :]
        fld[f, TILE + ABOVE : 2 * TILE, :] = ends[f, TILE : 2 * TILE - ABOVE, :]
    mine = own_columns(wide)
    low, low_cells = row_masks(wide, kept - EDGE_BOTTOM, kept - 1)
    high, high_cells = row_masks(wide, ABOVE, ABOVE + EDGE_TOP - 1)
    row = lax.broadcasted_iota(jnp.int32, (TILE, wide), 0)
    high = high | ((row == ABOVE - 1) & (lax.axis_index("gy") == 0))

    def put(t, which, value):
        if t == 0:
            edges[which, 2 * TILE - EDGE_BOTTOM : 2 * TILE, :] = value[kept - EDGE_BOTTOM : kept]
        else:
            edges[which, 0:EDGE_TOP, :] = value[ABOVE : ABOVE + EDGE_TOP]

    mixed = [theta[i][0:1, 0:1] for i in range(2)]
    made, _ = sweep(scratch, [[x & low for x in mine], [x & high for x in mine]], [low_cells, high_cells], mixed, put)
    row = lax.broadcasted_iota(jnp.int32, (2 * TILE, LANES), 0)
    stack = jnp.zeros((2 * TILE, LANES), jnp.float32)
    for i, value in enumerate(made):
        stack = jnp.where(row == i, jnp.sum(value + partial[i], axis=0, keepdims=True), stack)
    stack = jnp.sum(stack, axis=1, keepdims=True)
    for i in range(2):
        stack = jnp.where(row[:, 0:1] == len(made) + i, mixed[i], stack)
    lane = lax.broadcasted_iota(jnp.int32, (2 * TILE, LANES), 1)
    solve, which = row // SUMS, lax.rem(row, SUMS)
    place = jnp.where(row < 2 * SUMS, SOLVE * which + solve, SOLVE * SUMS + row - 2 * SUMS)
    line = jnp.sum(jnp.where(lane == place, stack, 0.0), axis=0, keepdims=True)
    sums[...] = jnp.broadcast_to(line, sums.shape)


def steps_of(table):
    def column(x, i):
        return pltpu.roll(x, (LANES - SOLVE * i) % LANES, 1)

    def over(x):
        return jnp.sum(x, axis=0, keepdims=True)

    used = lax.broadcasted_iota(jnp.int32, (1, LANES), 1) < 2
    norm_d, _, size, cross, ww, rw, rr, theta_d = [column(table, i) for i in range(SUMS + 1)]
    sums = over(table)
    norm, prod = [jnp.where(used, column(sums, i), 1.0) for i in range(2)]
    alpha = norm / prod
    shift = theta_d - prod / norm
    square = alpha * alpha
    norm_1 = square * over(size + shift * (2.0 * cross + shift * norm_d))
    prod_1 = square * over(ww + shift * (2.0 * rw + shift * rr))
    ratio = norm_1 / norm
    some = used & (norm_1 > 0.0)
    bottom = jnp.where(some, prod_1 - ratio * norm_1 / alpha, 1.0)
    return alpha, ratio, jnp.where(some, norm_1, 0.0) / bottom


def finish_kernel(table, own, vectors, edges, velocity, adjoint, grad):
    found = steps_of(table[...])
    steps = [[x[:, s : s + 1] for x in found] for s in range(2)]
    rows, cols = own.shape[1:]
    last = rows // TILE - 1
    row = lax.broadcasted_iota(jnp.int32, (TILE, cols), 0)
    for t in range(last + 1):
        at = pl.ds(TILE * t, TILE)

        def vector(which):
            x = vectors[which, at, :]
            if t == 0:
                x = jnp.where(row < EDGE_TOP, edges[which, 0:TILE, :], x)
            if t == last:
                x = jnp.where(row >= TILE - EDGE_BOTTOM, edges[which, TILE : 2 * TILE, :], x)
            return x

        made = []
        for s in range(2):
            alpha, ratio, alpha_1 = steps[s]
            for i in range(2):
                r, q = vector(4 * s + i), vector(4 * s + 2 + i)
                step = alpha * r + alpha_1 * ((r - alpha * q) + ratio * r)
                made.append(own[i, at, :] + step if s == 0 else step)
        friction = jnp.where(own[2, at, :] > 0.0, own[3, at, :], 0.0)
        velocity[0, at, :], velocity[1, at, :] = made[0], made[1]
        adjoint[0, at, :], adjoint[1, at, :] = made[2], made[3]
        grad[at, :] = -friction * (made[0] * made[2] + made[1] * made[3])


def shape(*dims):
    return jax.ShapeDtypeStruct(dims, jnp.float32)


def call(kernel, outs, scratch=(), **kwargs):
    return pl.pallas_call(
        kernel,
        out_shape=outs,
        scratch_shapes=scratch,
        compiler_params=pltpu.CompilerParams(vmem_limit_bytes=VMEM_LIMIT),
        **kwargs,
    )


def sweep_scratch(tiles, wide):
    rows = TILE * tiles
    deep = [pltpu.VMEM((n, rows + TILE, wide), jnp.float32) for n in (FIELDS, 9, 4, 4)]
    return [deep[0], pltpu.VMEM((rows, wide), jnp.float32), *deep[1:], pltpu.VMEM((6, rows, wide), jnp.float32)]


def swap(x, axis, first):
    pairs = [(i, i + 1) for i in range(first, lax.axis_size(axis) - 1, 2)]
    return lax.ppermute(x, axis, pairs + [(j, i) for i, j in pairs])


def shards(ice_mask, grounded, thickness, friction, previous_velocity, observed, driving):
    raw = (ice_mask, grounded, thickness, friction, previous_velocity, observed, driving)
    rows, cols = ice_mask.shape
    wide, tiles = cols + LANES, rows // TILE
    devices = lax.axis_size(("gy", "gx"))
    own, sends = call(
        pack_kernel,
        (shape(FIELDS, rows, cols), shape(lax.axis_size("gx") * TILE * block_tiles(rows), LANES)),
        scratch=[pltpu.VMEM(x.shape, x.dtype) for x in raw] + [pltpu.SemaphoreType.DMA((len(raw),))],
        in_specs=[pl.BlockSpec(memory_space=pltpu.HBM)] * len(raw),
        name="pack",
    )(*[pltpu.with_memory_space_constraint(x, pltpu.HBM) for x in raw])
    columns = lax.all_to_all(sends, "gx", 0, 0, tiled=True)
    ends, across, beside = call(
        rows_kernel,
        (shape(FIELDS, 2 * TILE, wide), shape(BELOW * FIELDS, wide), shape(BELOW * FIELDS, wide)),
        name="rows",
    )(own, columns)
    across = swap(across, "gy", 1)
    beside = swap(beside, "gy", 0)
    vectors, partial, theta = call(
        inner_kernel,
        (
            shape(8, rows, cols),
            shape(2 * SUMS, TILE, LANES),
            shape(2, TILE, LANES),
        ),
        scratch=sweep_scratch(tiles, wide),
        cost_estimate=pl.CostEstimate(flops=500 * rows * wide, bytes_accessed=64 * rows * wide, transcendentals=0),
        name="inner",
    )(own, columns)
    edges, sums = call(
        outer_kernel,
        (shape(8, 2 * TILE, cols), shape(devices, LANES)),
        scratch=sweep_scratch(2, wide),
        name="outer",
    )(ends, across, beside, partial, theta)
    table = lax.all_to_all(sums, ("gy", "gx"), 0, 0, tiled=True)
    return call(
        finish_kernel,
        (shape(2, rows, cols), shape(2, rows, cols), shape(rows, cols)),
        name="finish",
    )(table, own, vectors, edges)


def solution(mesh):
    flat, both = P("gy", "gx"), P(None, "gy", "gx")
    return jax.shard_map(
        shards,
        mesh=mesh,
        in_specs=(flat, flat, flat, flat, both, both, both),
        out_specs=(both, both, flat),
        check_vma=False,
    )
```
